32 devices in a mesh: band: 8 (over y, x, core), grid: 4 (over z).
Axes of the slice: x: 2, y: 2, z: 4, core: 2. Of those that a mesh axis runs over, the one named last changes fastest.
Arguments:
- own_orbitals: bfloat16 [16, 128, 128, 128], P('band', 'grid'), may hold values from -9 to 9
- resident_orbitals: bfloat16 [16, 128, 128, 128], P('band', 'grid'), may hold values from -9 to 9
- pair_lists: int32 [8, 2, 2, 2], P('band'), may hold values from 0 to 1, as said below
- pair_counts: int32 [8, 2], P('band'), may hold values from 1 to 2, as said below
Outputs:
- exchange_block: bfloat16 [16, 128, 128, 128], P('band', 'grid')
- intersection: float32 [16, 2], P('band')
The draws below stay inside these ranges and needn't reach their ends.
Inputs may be any that keep to these rules, and one draw needn't show every extreme that they name: pair_lists[b, l, s] = (i, j) pairs band i of block b with band j of the partner block of list l; the 2 pairs of one list are distinct; slots s >= pair_counts[b, l] hold pairs that are not used. `pair_counts`: in each of the two lists exactly one block has 2 live slots, every other block exactly 1.
All inputs are finite; a program needn't handle non-finite values.
Results may differ from the reference program's by a relative error of at most 0.00045.
Values may be sent and summed in bfloat16 or wider, within the bound.
A program may use at most 64 MiB of HBM per device.

```python
import jax
import jax.numpy as jnp
from jax import lax

NG = 128
BANDS_DEV = 2
PAIRS = 2
BLOCKS = 8
BANDS = 16


def orbital_field(key, salt):
    subkey = jax.random.fold_in(key, salt)
    planes = jnp.arange(NG, dtype=jnp.float32) / NG
    envelope = (0.6 * 3.0 ** planes)[None, :, None, None]
    noise = jnp.clip(jax.random.normal(subkey, (BANDS, NG, NG, NG), jnp.float32), -5.0, 5.0)
    field = envelope * noise
    return field.astype(jnp.bfloat16)


def draw_own_orbitals(key, part):
    return orbital_field(key, 4101)


def draw_resident_orbitals(key, part):
    return orbital_field(key, 4202)


def pair_tables(key):
    base = jax.random.fold_in(key, 7001)
    count_key, hot_key, perm_key = jax.random.split(base, 3)
    light = jax.random.randint(count_key, (BLOCKS, 2), 1, PAIRS, dtype=jnp.int32)
    hottest = jax.random.randint(hot_key, (2,), 0, BLOCKS, dtype=jnp.int32)
    block_ids = jnp.arange(BLOCKS, dtype=jnp.int32)
    counts = jnp.where(block_ids[:, None] == hottest[None, :], PAIRS, light).astype(jnp.int32)
    list_keys = jax.random.split(perm_key, BLOCKS * 2)

    def pick_codes(subkey):
        return jax.random.permutation(subkey, BANDS_DEV * BANDS_DEV)[:PAIRS]
    codes = jax.vmap(pick_codes)(list_keys).reshape(BLOCKS, 2, PAIRS).astype(jnp.int32)
    pairs = jnp.stack([codes // BANDS_DEV, codes % BANDS_DEV], axis=-1).astype(jnp.int32)
    return (pairs, counts)


def draw_pair_lists(key, part):
    return pair_tables(key)[0]


def draw_pair_counts(key, part):
    return pair_tables(key)[1]


def setup_inputs(seed: int = 0) -> dict:
    key_of = jax.random.split(jax.random.key(seed), 5)
    own_orbitals = draw_own_orbitals(jax.random.fold_in(key_of[4], 71), 0)
    resident_orbitals = draw_resident_orbitals(jax.random.fold_in(key_of[4], 71), 0)
    pair_lists = draw_pair_lists(jax.random.fold_in(key_of[4], 71), 0)
    pair_counts = draw_pair_counts(jax.random.fold_in(key_of[4], 71), 0)
    return {"own_orbitals": own_orbitals, "resident_orbitals": resident_orbitals, "pair_lists": pair_lists, "pair_counts": pair_counts}


def fold_freq(indices, length):
    return jnp.minimum(indices, length - indices).astype(jnp.float32)


def coulomb(first_freq, middle_freq, last_freq, length):
    squared = (fold_freq(first_freq, length)[:, None, None] ** 2
               + fold_freq(middle_freq, length)[None, :, None] ** 2
               + fold_freq(last_freq, length)[None, None, :] ** 2)
    return jnp.where(squared > 0.5, 0.25 * length ** 1.5 / jnp.maximum(squared, 1.0), 0.0)


def poisson(density, kernel):
    spectrum = jnp.fft.rfftn(density)
    return jnp.fft.irfftn(spectrum * kernel, s=density.shape).astype(jnp.float32)


def reference(own_orbitals, resident_orbitals, pair_lists, pair_counts):
    received = jnp.roll(resident_orbitals, BANDS_DEV, axis=0)
    kernel = coulomb(jnp.arange(NG, dtype=jnp.int32), jnp.arange(NG, dtype=jnp.int32),
                     jnp.arange(NG // 2 + 1, dtype=jnp.int32), NG)
    band_ids = jnp.arange(BANDS_DEV, dtype=jnp.int32)

    def one_block(inputs):
        own_block, resident_block, received_block, list_block, count_block = inputs
        running_sum = jnp.zeros(own_block.shape, jnp.float32)
        for list_index, partners in ((0, resident_block), (1, received_block)):
            for slot_index in range(PAIRS):
                first_band = list_block[list_index, slot_index, 0]
                second_band = list_block[list_index, slot_index, 1]
                partner_row = lax.dynamic_index_in_dim(partners, second_band, 0, keepdims=False).astype(jnp.float32)
                own_row = lax.dynamic_index_in_dim(own_block, first_band, 0, keepdims=False).astype(jnp.float32)
                potential = poisson(own_row * partner_row, kernel)
                live_weight = (slot_index < count_block[list_index]).astype(jnp.float32)
                weights = (band_ids == first_band).astype(jnp.float32) * live_weight
                running_sum = running_sum + weights[:, None, None, None] * (potential * partner_row)[None]
        intersection = jnp.dot(own_block.reshape(BANDS_DEV, -1).astype(jnp.float32),
                          running_sum.reshape(BANDS_DEV, -1).T, precision=lax.Precision.HIGHEST)
        return running_sum.astype(jnp.bfloat16), intersection

    shape_blocks = (BLOCKS, BANDS_DEV, NG, NG, NG)
    exchange_all, intersection_all = lax.map(one_block, (own_orbitals.reshape(shape_blocks),
                                                    resident_orbitals.reshape(shape_blocks),
                                                    received.reshape(shape_blocks),
                                                    pair_lists, pair_counts))
    return exchange_all.reshape(BANDS, NG, NG, NG), intersection_all.reshape(BANDS, BANDS_DEV)
```

```python
import functools
import math

import jax
import jax.numpy as jnp
import numpy as np
import ml_dtypes
from jax import lax
from jax.experimental import pallas as pl
from jax.experimental.pallas import tpu as pltpu
from jax.sharding import PartitionSpec as P

F32 = jnp.float32
BF16 = jnp.bfloat16
I16 = jnp.int16
MESH = pl.DeviceIdType.MESH
FINE_ROWS = 16
FINE = 65000.0
TOP = 32700.0
LIMIT = 56 * 2**20


def tables(length, parts):
    k = np.arange(length)
    angles = (np.outer(k, k) % length) * (2.0 * math.pi / length)
    cas = (np.cos(angles) + np.sin(angles)) / math.sqrt(length)
    order = sorted(range(length), key=lambda i: (min(i, length - i), i))
    rows = length // parts
    perm = np.array([order[r * parts + g] for g in range(parts) for r in range(rows)])

    def split(m):
        high = m.astype(np.float32).astype(ml_dtypes.bfloat16)
        low = (m - high.astype(np.float64)).astype(np.float32).astype(ml_dtypes.bfloat16)
        return high, low

    def left(m):
        high, low = split(m)
        return np.block([[high, high], [low, np.zeros_like(low)]])

    def right(m):
        high, low = split(m)
        return np.block([[high, low], [high, np.zeros_like(low)]])

    return [
        jnp.asarray(t.astype(ml_dtypes.bfloat16))
        for t in (right(cas), left(cas[perm, :]), left(cas), left(cas[:, perm]))
    ]


def halves(v):
    high = v.astype(BF16)
    return high, (v - high.astype(F32)).astype(BF16)


def times_right(v, table):
    high, low = halves(v)
    n = v.shape[1]
    out = jnp.dot(jnp.concatenate([high, low], 1), table, preferred_element_type=F32)
    return out[:, :n] + out[:, n:]


def times_left(table, a, b):
    ah, al = halves(a)
    bh, bl = halves(b)
    rhs = jnp.concatenate(
        [jnp.concatenate([ah, bh], 1), jnp.concatenate([al, bl], 1)], 0
    )
    out = jnp.dot(table, rhs, preferred_element_type=F32)
    n = a.shape[0]
    return out[:n] + out[n:]


def tile_max(running, v):
    return jnp.maximum(running, jnp.max(jnp.abs(v).reshape(-1, 8, v.shape[-1]), axis=0))


def folded(index, length):
    return jnp.minimum(index, length - index)


def code_of(peak):
    peak = jnp.maximum(jnp.max(peak, keepdims=True), 1e-30)
    return jnp.ceil(jnp.log2(peak) * 256.0)


def size_of(code):
    return jnp.exp2(code * (1.0 / 256.0))


class Sizes:
    def __init__(self, bands, planes, length):
        self.bands = bands
        self.planes = planes
        self.length = length
        self.parts = length // planes
        self.rows = planes
        self.fine = max(2, FINE_ROWS // self.parts)
        self.all_rows = self.rows + self.fine + 1
        self.group = min(8, self.rows)

    def coded(self):
        return (self.parts, self.all_rows, self.planes, self.length)


def write_words(sz, out, where, base, load, inverse, code):
    def words(v):
        return v.astype(jnp.int32).astype(I16)

    def body(r, _):
        out[where, r] = words(jnp.round(load(r) * inverse))
        return 0

    for r in range(sz.fine):
        scaled = load(r) * inverse
        whole = jnp.round(scaled)
        out[where, r] = words(whole)
        out[where, sz.rows + r] = words(jnp.round((scaled - whole) * FINE))
    lax.fori_loop(sz.fine, sz.rows, body, 0, unroll=2)
    out[where, sz.rows + sz.fine] = words(
        jnp.broadcast_to(code, (sz.planes, sz.length))
    )


def forward(sz, own, partner, wz, wy, t):
    n = sz.length

    def body(step, peak):
        x = step * 4
        d = own(x, 4).astype(F32) * partner(x, 4).astype(F32)
        e = times_right(d.reshape(4 * n, n), wz[...])
        for h in range(2):
            a, b = 2 * h, 2 * h + 1
            f = times_left(wy[...], e[a * n : (a + 1) * n], e[b * n : (b + 1) * n])
            t[pl.ds(x + a, n, stride=sz.planes), :] = f[:, :n]
            t[pl.ds(x + b, n, stride=sz.planes), :] = f[:, n:]
            peak = tile_max(peak, f)
        return peak

    return lax.fori_loop(0, sz.planes // 4, body, jnp.zeros((8, 2 * n), F32))


def forward_words(sz, t, out, where, code):
    inverse = TOP / size_of(code)
    base = where * (sz.rows * sz.planes)

    def load(r):
        start = pl.multiple_of(base + r * sz.planes, sz.planes)
        return t[pl.ds(start, sz.planes), :]

    write_words(sz, out, where, base, load, inverse, code)


def set_scales(sz, coded, scales):
    for src in range(sz.parts):
        row = coded[src, sz.rows + sz.fine].astype(jnp.int32).astype(F32)
        scales[src * sz.planes : (src + 1) * sz.planes, :] = size_of(row) * (1.0 / TOP)


def numbers(sz, coded, src, r, is_fine):
    v = coded[src, r].astype(jnp.int32).astype(F32)
    if is_fine:
        v = v + coded[src, sz.rows + r].astype(jnp.int32).astype(F32) * (1.0 / FINE)
    return v


def row_frequency(sz, part, r):
    return ((r * sz.parts + part + 1) // 2).astype(F32)


def column_power(sz, my, power):
    kz = folded(lax.broadcasted_iota(jnp.int32, (8, sz.length), 1), sz.length).astype(F32)
    squared = jnp.maximum(kz * kz + my * my, 1.0)
    root = jnp.sqrt(squared)
    w = root * jnp.sqrt(root)
    return (w if power > 0 else 1.0 / w)[0:1]


def middle(sz, me, coded, wx, scales, u):
    n = sz.length
    set_scales(sz, coded, scales)
    factor = 0.25 * n**1.5

    def squares():
        kx = folded(lax.broadcasted_iota(jnp.int32, (n, n), 0), n)
        kz = folded(lax.broadcasted_iota(jnp.int32, (n, n), 1), n)
        return (kx * kx + kz * kz).astype(F32)

    def pair(r, is_fine, peak):
        g = [
            jnp.concatenate(
                [numbers(sz, coded, src, r + h, is_fine) for src in range(sz.parts)], 0
            )
            * scales[...]
            for h in range(2)
        ]
        s = times_left(wx[...], g[0], g[1])
        base = squares()
        filtered = []
        my = [row_frequency(sz, me, jnp.int32(r) + h) for h in range(2)]
        for h in range(2):
            k = base + my[h] * my[h]
            k = jnp.where(k > 0.5, factor / jnp.maximum(k, 1.0), 0.0)
            filtered.append(s[:, h * n : (h + 1) * n] * k)
        back = times_left(wx[...], filtered[0], filtered[1])
        for h in range(2):
            v = back[:, h * n : (h + 1) * n] * column_power(sz, my[h], 1)
            u[r + h] = v
            peak = tile_max(peak, v)
        return peak

    peak = jnp.zeros((8, n), F32)
    for r in range(0, sz.fine, 2):
        peak = pair(r, True, peak)
    return lax.fori_loop(
        sz.fine // 2, sz.rows // 2, lambda s, p: pair(s * 2, False, p), peak
    )


def middle_words(sz, u, out, where, code):
    inverse = TOP / size_of(code)

    def load(r):
        return u[r, pl.ds(pl.multiple_of(where * sz.planes, sz.planes), sz.planes), :]

    write_words(sz, out, where, None, load, inverse, code)


def backward(sz, coded, wz, wyi, scales, t, partner, add):
    n = sz.length
    set_scales(sz, coded, scales)
    for src in range(sz.parts):

        def put(r, is_fine):
            my = row_frequency(sz, src, jnp.int32(r))
            scale = scales[src * sz.planes : src * sz.planes + 8, :][0:1]
            v = numbers(sz, coded, src, r, is_fine) * (scale * column_power(sz, my, -1))
            start = pl.multiple_of((src * sz.rows + r) * sz.planes, sz.planes)
            t[pl.ds(start, sz.planes), :] = v

        for r in range(sz.fine):
            put(r, True)

        def body(r, _):
            put(r, False)
            return 0

        lax.fori_loop(sz.fine, sz.rows, body, 0, unroll=2)

    def planes(step, _):
        x = step * 2
        a = t[pl.ds(x, n, stride=sz.planes), :]
        b = t[pl.ds(x + 1, n, stride=sz.planes), :]
        f = times_left(wyi[...], a, b)
        v = times_right(jnp.concatenate([f[:, :n], f[:, n:]], 0), wz[...])
        add(x, v.reshape(2, n, n) * partner(x, 2).astype(F32))
        return 0

    lax.fori_loop(0, sz.planes // 2, planes, 0, unroll=2)


def regular_kernel(
    sz, lists, own, resident, wz, wy, wx, wyi, total, received,
    arrived, t, u, scales, out1, in1, out2, in2,
    send_sem, recv_sem, pass_send, pass_recv, local_sem, save_sem,
):
    me = lax.axis_index("grid")
    block = lax.axis_index("band")
    blocks = lax.axis_size("band")
    parts = sz.parts
    after = lax.rem(block + 1, blocks)
    before = lax.rem(block + blocks - 1, blocks)

    barrier = pltpu.get_barrier_semaphore()
    for o in range(1, parts):
        pl.semaphore_signal(
            barrier, inc=1, device_id=(block, lax.rem(me + o, parts)), device_id_type=MESH
        )
    for other in (after, before):
        pl.semaphore_signal(barrier, inc=1, device_id=(other, me), device_id_type=MESH)
    pl.semaphore_wait(barrier, parts + 1)

    passing = pltpu.make_async_remote_copy(
        src_ref=resident, dst_ref=arrived, send_sem=pass_send, recv_sem=pass_recv,
        device_id=(after, me), device_id_type=MESH,
    )
    passing.start()

    firsts = [lists[0, l, 0, 0] for l in range(2)]
    seconds = [lists[0, l, 0, 1] for l in range(2)]
    partners = (resident, arrived)

    def remote(phase, src, dst, l, o):
        to = lax.rem(me + o, parts)
        return pltpu.make_async_remote_copy(
            src_ref=src.at[l, to], dst_ref=dst.at[l, me],
            send_sem=send_sem.at[phase, l, o], recv_sem=recv_sem.at[phase, l, o],
            device_id=(block, to), device_id_type=MESH,
        )

    def send(phase, src, dst, l, write):
        copies = []
        for o in range(1, parts):
            write(lax.rem(me + o, parts))
            c = remote(phase, src, dst, l, o)
            c.start()
            copies.append(c)
        write(me)
        c = pltpu.make_async_copy(src.at[l, me], dst.at[l, me], local_sem.at[phase, l])
        c.start()
        copies.append(c)
        return copies

    flights = {}
    for l in range(2):
        if l == 1:
            passing.wait()
            saving = pltpu.make_async_copy(arrived, received, save_sem)
            saving.start()
        peak = forward(
            sz,
            lambda x, c: own[firsts[l], pl.ds(x, c)],
            lambda x, c: partners[l][seconds[l], pl.ds(x, c)],
            wz, wy, t,
        )
        code = code_of(peak)
        flights[0, l] = send(
            0, out1, in1, l, lambda w: forward_words(sz, t, out1.at[l], w, code)
        )
    for l in range(2):
        for c in flights[0, l]:
            c.wait()
        code = code_of(middle(sz, me, in1.at[l], wx, scales, u))
        flights[1, l] = send(
            1, out2, in2, l, lambda w: middle_words(sz, u, out2.at[l], w, code)
        )
    for l in range(2):
        for c in flights[1, l]:
            c.wait()

        def add(x, v):
            for band in range(sz.bands):
                share = v * (firsts[l] == band).astype(F32)
                if l == 0:
                    total[band, pl.ds(x, 2)] = share
                else:
                    total[band, pl.ds(x, 2)] += share

        backward(
            sz, in2.at[l], wz, wyi, scales, t,
            lambda x, c: partners[l][seconds[l], pl.ds(x, c)], add,
        )
    saving.wait()


def regular(sz, lists, own, resident, wz, wy, wx, wyi):
    n = sz.length
    vmem = pl.BlockSpec(memory_space=pltpu.VMEM)
    coded = pltpu.VMEM((2,) + sz.coded(), I16)
    return pl.pallas_call(
        functools.partial(regular_kernel, sz),
        out_shape=(
            jax.ShapeDtypeStruct(own.shape, F32),
            jax.ShapeDtypeStruct(own.shape, BF16),
        ),
        in_specs=[pl.BlockSpec(memory_space=pltpu.SMEM)] + [vmem] * 6,
        out_specs=(vmem, pl.BlockSpec(memory_space=pl.ANY)),
        scratch_shapes=[
            pltpu.VMEM(own.shape, BF16),
            pltpu.VMEM((n * sz.planes, n), F32),
            pltpu.VMEM((sz.rows, n, n), F32),
            pltpu.VMEM((n, n), F32),
            coded, coded, coded, coded,
            pltpu.SemaphoreType.DMA((2, 2, sz.parts)),
            pltpu.SemaphoreType.DMA((2, 2, sz.parts)),
            pltpu.SemaphoreType.DMA,
            pltpu.SemaphoreType.DMA,
            pltpu.SemaphoreType.DMA((2, 2)),
            pltpu.SemaphoreType.DMA,
        ],
        compiler_params=pltpu.CompilerParams(
            collective_id=0, has_side_effects=True, vmem_limit_bytes=LIMIT
        ),
        name="regular_pairs",
    )(lists, own, resident, wz, wy, wx, wyi)


def extra_forward(sz, own, partner, wz, wy):
    def kernel(own_ref, partner_ref, wz_ref, wy_ref, out, t):
        peak = forward(
            sz, lambda x, c: own_ref[pl.ds(x, c)], lambda x, c: partner_ref[pl.ds(x, c)],
            wz_ref, wy_ref, t,
        )
        code = code_of(peak)
        for g in range(sz.parts):
            forward_words(sz, t, out, g, code)

    return pl.pallas_call(
        kernel,
        out_shape=jax.ShapeDtypeStruct(sz.coded(), I16),
        scratch_shapes=[pltpu.VMEM((sz.length * sz.planes, sz.length), F32)],
        compiler_params=pltpu.CompilerParams(vmem_limit_bytes=LIMIT),
        name="extra_forward",
    )(own, partner, wz, wy)


def extra_middle(sz, coded, wx):
    n = sz.length

    def kernel(coded_ref, wx_ref, out, scales, u):
        me = lax.axis_index("grid")
        code = code_of(middle(sz, me, coded_ref, wx_ref, scales, u))
        for g in range(sz.parts):
            middle_words(sz, u, out, g, code)

    return pl.pallas_call(
        kernel,
        out_shape=jax.ShapeDtypeStruct(sz.coded(), I16),
        scratch_shapes=[pltpu.VMEM((n, n), F32), pltpu.VMEM((sz.rows, n, n), F32)],
        compiler_params=pltpu.CompilerParams(vmem_limit_bytes=LIMIT),
        name="extra_middle",
    )(coded, wx)


def extra_backward(sz, coded, partner, wz, wyi):
    n = sz.length

    def kernel(coded_ref, partner_ref, wz_ref, wyi_ref, out, scales, t):
        def add(x, v):
            out[pl.ds(x, 2)] = v

        backward(
            sz, coded_ref, wz_ref, wyi_ref, scales, t,
            lambda x, c: partner_ref[pl.ds(x, c)], add,
        )

    return pl.pallas_call(
        kernel,
        out_shape=jax.ShapeDtypeStruct((sz.planes, n, n), F32),
        scratch_shapes=[pltpu.VMEM((n, n), F32), pltpu.VMEM((n * sz.planes, n), F32)],
        compiler_params=pltpu.CompilerParams(vmem_limit_bytes=LIMIT),
        name="extra_backward",
    )(coded, partner, wz, wyi)


def finish(sz, own, total):
    def kernel(own_ref, total_ref, out, products):
        t = pl.program_id(0)

        @pl.when(t == 0)
        def _():
            products[...] = jnp.zeros_like(products)

        out[...] = total_ref[...].astype(BF16)
        for i in range(sz.bands):
            for k in range(sz.bands):
                v = own_ref[i].astype(F32) * total_ref[k]
                products[i, k] += jnp.sum(v.reshape(-1, 8, sz.length), axis=0)

    step = 4
    spec = pl.BlockSpec(
        (sz.bands, step, sz.length, sz.length), lambda t: (0, t, 0, 0)
    )
    shape = (sz.bands, sz.bands, 8, sz.length)
    return pl.pallas_call(
        kernel,
        grid=(sz.planes // step,),
        in_specs=[spec, spec],
        out_specs=(spec, pl.BlockSpec(shape, lambda t: (0, 0, 0, 0))),
        out_shape=(
            jax.ShapeDtypeStruct(own.shape, BF16),
            jax.ShapeDtypeStruct(shape, F32),
        ),
        compiler_params=pltpu.CompilerParams(vmem_limit_bytes=LIMIT),
        name="finish",
    )(own, total)


def on_device(own, resident, pair_lists, pair_counts):
    bands, planes, length, _ = own.shape
    sz = Sizes(bands, planes, length)
    wz, wy, wx, wyi = tables(length, sz.parts)
    total, received = regular(sz, pair_lists, own, resident, wz, wy, wx, wyi)
    extras = pair_counts[0] - 1

    def one_pair(step, running):
        l = (step >= extras[0]).astype(jnp.int32)
        slot = 1 + step - l * extras[0]
        row = pair_lists[0, l, slot]
        own_band = lax.dynamic_index_in_dim(own, row[0], 0, keepdims=False)
        partner = jnp.where(
            l == 0,
            lax.dynamic_index_in_dim(resident, row[1], 0, keepdims=False),
            lax.dynamic_index_in_dim(received, row[1], 0, keepdims=False),
        )
        coded = extra_forward(sz, own_band, partner, wz, wy)
        coded = lax.all_to_all(coded, "grid", split_axis=0, concat_axis=0, tiled=True)
        coded = extra_middle(sz, coded, wx)
        coded = lax.all_to_all(coded, "grid", split_axis=0, concat_axis=0, tiled=True)
        term = extra_backward(sz, coded, partner, wz, wyi)
        old = lax.dynamic_index_in_dim(running, row[0], 0, keepdims=False)
        return lax.dynamic_update_index_in_dim(running, old + term, row[0], 0)

    total = lax.fori_loop(0, extras[0] + extras[1], one_pair, total)
    rounded, products = finish(sz, own, total)
    return rounded, lax.psum(jnp.sum(products, axis=(2, 3)), "grid")


def solution(mesh):
    in_specs = (
        P("band", "grid", None, None),
        P("band", "grid", None, None),
        P("band", None, None, None),
        P("band", None),
    )
    out_specs = (P("band", "grid", None, None), P("band", None))
    return jax.shard_map(
        on_device, mesh=mesh, in_specs=in_specs, out_specs=out_specs, check_vma=False
    )
```

```python
import functools
import math

import jax
import jax.numpy as jnp
import numpy as np
import ml_dtypes
from jax import lax
from jax.experimental import pallas as pl
from jax.experimental.pallas import tpu as pltpu
from jax.sharding import PartitionSpec as P

F32 = jnp.float32
BF16 = jnp.bfloat16
I16 = jnp.int16
MESH = pl.DeviceIdType.MESH
FINE_ROWS = 8
FINE = 65000.0
TOP = 32700.0
LIMIT = 56 * 2**20


def tables(length, parts):
    k = np.arange(length)
    angles = (np.outer(k, k) % length) * (2.0 * math.pi / length)
    cas = (np.cos(angles) + np.sin(angles)) / math.sqrt(length)
    order = sorted(range(length), key=lambda i: (min(i, length - i), i))
    rows = length // parts
    perm = np.array([order[r * parts + g] for g in range(parts) for r in range(rows)])

    def split(m):
        high = m.astype(np.float32).astype(ml_dtypes.bfloat16)
        low = (m - high.astype(np.float64)).astype(np.float32).astype(ml_dtypes.bfloat16)
        return high, low

    def left(m):
        high, low = split(m)
        return np.block([[high, high], [low, np.zeros_like(low)]])

    def right(m):
        high, low = split(m)
        return np.block([[high, low], [high, np.zeros_like(low)]])

    return [
        jnp.asarray(t.astype(ml_dtypes.bfloat16))
        for t in (right(cas), left(cas[perm, :]), left(cas), left(cas[:, perm]))
    ]


def halves(v):
    high = v.astype(BF16)
    return high, (v - high.astype(F32)).astype(BF16)


def times_right(v, table):
    high, low = halves(v)
    n = v.shape[1]
    out = jnp.dot(jnp.concatenate([high, low], 1), table, preferred_element_type=F32)
    return out[:, :n] + out[:, n:]


def times_left(table, a, b):
    ah, al = halves(a)
    bh, bl = halves(b)
    rhs = jnp.concatenate(
        [jnp.concatenate([ah, bh], 1), jnp.concatenate([al, bl], 1)], 0
    )
    out = jnp.dot(table, rhs, preferred_element_type=F32)
    n = a.shape[0]
    return out[:n] + out[n:]


def tile_max(running, v):
    return jnp.maximum(running, jnp.max(jnp.abs(v).reshape(-1, 8, v.shape[-1]), axis=0))


def folded(index, length):
    return jnp.minimum(index, length - index)


def code_of(peak):
    peak = jnp.maximum(jnp.max(peak, keepdims=True), 1e-30)
    return jnp.ceil(jnp.log2(peak) * 256.0)


def size_of(code):
    return jnp.exp2(code * (1.0 / 256.0))


class Sizes:
    def __init__(self, bands, planes, length):
        self.bands = bands
        self.planes = planes
        self.length = length
        self.parts = length // planes
        self.rows = planes
        self.fine = max(2, FINE_ROWS // self.parts)
        self.all_rows = self.rows + self.fine + 1
        self.group = min(8, self.rows)

    def coded(self):
        return (self.parts, self.all_rows, self.planes, self.length)


def write_words(sz, out, where, base, load, inverse, code):
    def words(v):
        return v.astype(jnp.int32).astype(I16)

    def body(r, _):
        out[where, r] = words(jnp.round(load(r) * inverse))
        return 0

    for r in range(sz.fine):
        scaled = load(r) * inverse
        whole = jnp.round(scaled)
        out[where, r] = words(whole)
        out[where, sz.rows + r] = words(jnp.round((scaled - whole) * FINE))
    lax.fori_loop(sz.fine, sz.rows, body, 0, unroll=2)
    out[where, sz.rows + sz.fine] = words(
        jnp.broadcast_to(code, (sz.planes, sz.length))
    )


def forward(sz, own, partner, wz, wy, t):
    n = sz.length

    def body(step, peak):
        x = step * 4
        d = own(x, 4).astype(F32) * partner(x, 4).astype(F32)
        e = times_right(d.reshape(4 * n, n), wz[...])
        for h in range(2):
            a, b = 2 * h, 2 * h + 1
            f = times_left(wy[...], e[a * n : (a + 1) * n], e[b * n : (b + 1) * n])
            t[pl.ds(x + a, n, stride=sz.planes), :] = f[:, :n]
            t[pl.ds(x + b, n, stride=sz.planes), :] = f[:, n:]
            peak = tile_max(peak, f)
        return peak

    return lax.fori_loop(0, sz.planes // 4, body, jnp.zeros((8, 2 * n), F32))


def forward_words(sz, t, out, where, code):
    inverse = TOP / size_of(code)
    base = where * (sz.rows * sz.planes)

    def load(r):
        start = pl.multiple_of(base + r * sz.planes, sz.planes)
        return t[pl.ds(start, sz.planes), :]

    write_words(sz, out, where, base, load, inverse, code)


def set_scales(sz, coded, scales):
    for src in range(sz.parts):
        row = coded[src, sz.rows + sz.fine].astype(jnp.int32).astype(F32)
        scales[src * sz.planes : (src + 1) * sz.planes, :] = size_of(row) * (1.0 / TOP)


def numbers(sz, coded, src, r, is_fine):
    v = coded[src, r].astype(jnp.int32).astype(F32)
    if is_fine:
        v = v + coded[src, sz.rows + r].astype(jnp.int32).astype(F32) * (1.0 / FINE)
    return v


def row_frequency(sz, part, r):
    return ((r * sz.parts + part + 1) // 2).astype(F32)


def column_power(sz, my, power):
    kz = folded(lax.broadcasted_iota(jnp.int32, (8, sz.length), 1), sz.length).astype(F32)
    squared = jnp.maximum(kz * kz + my * my, 1.0)
    root = jnp.sqrt(squared)
    w = root * jnp.sqrt(root)
    return (w if power > 0 else 1.0 / w)[0:1]


def middle(sz, me, coded, wx, scales, u):
    n = sz.length
    set_scales(sz, coded, scales)
    factor = 0.25 * n**1.5

    def squares():
        kx = folded(lax.broadcasted_iota(jnp.int32, (n, n), 0), n)
        kz = folded(lax.broadcasted_iota(jnp.int32, (n, n), 1), n)
        return (kx * kx + kz * kz).astype(F32)

    def pair(r, is_fine, peak):
        g = [
            jnp.concatenate(
                [numbers(sz, coded, src, r + h, is_fine) for src in range(sz.parts)], 0
            )
            * scales[...]
            for h in range(2)
        ]
        s = times_left(wx[...], g[0], g[1])
        base = squares()
        filtered = []
        my = [row_frequency(sz, me, jnp.int32(r) + h) for h in range(2)]
        for h in range(2):
            k = base + my[h] * my[h]
            k = jnp.where(k > 0.5, factor / jnp.maximum(k, 1.0), 0.0)
            filtered.append(s[:, h * n : (h + 1) * n] * k)
        back = times_left(wx[...], filtered[0], filtered[1])
        for h in range(2):
            v = back[:, h * n : (h + 1) * n] * column_power(sz, my[h], 1)
            u[r + h] = v
            peak = tile_max(peak, v)
        return peak

    peak = jnp.zeros((8, n), F32)
    for r in range(0, sz.fine, 2):
        peak = pair(r, True, peak)
    return lax.fori_loop(
        sz.fine // 2, sz.rows // 2, lambda s, p: pair(s * 2, False, p), peak
    )


def middle_words(sz, u, out, where, code):
    inverse = TOP / size_of(code)

    def load(r):
        return u[r, pl.ds(pl.multiple_of(where * sz.planes, sz.planes), sz.planes), :]

    write_words(sz, out, where, None, load, inverse, code)


def backward(sz, coded, wz, wyi, scales, t, partner, add, start=0):
    n = sz.length
    set_scales(sz, coded, scales)
    for src in range(sz.parts):

        def put(r, is_fine):
            my = row_frequency(sz, src, jnp.int32(r))
            scale = scales[src * sz.planes : src * sz.planes + 8, :][0:1]
            v = numbers(sz, coded, src, r, is_fine) * (scale * column_power(sz, my, -1))
            first = pl.multiple_of((src * sz.rows + r) * sz.planes, sz.planes)
            t[pl.ds(first, sz.planes), :] = v

        for r in range(sz.fine):
            put(r, True)

        def body(r, _):
            put(r, False)
            return 0

        lax.fori_loop(sz.fine, sz.rows, body, 0, unroll=2)

    def planes(step, carried):
        x = step * 2
        a = t[pl.ds(x, n, stride=sz.planes), :]
        b = t[pl.ds(x + 1, n, stride=sz.planes), :]
        f = times_left(wyi[...], a, b)
        v = times_right(jnp.concatenate([f[:, :n], f[:, n:]], 0), wz[...])
        return add(x, v.reshape(2, n, n) * partner(x, 2).astype(F32), carried)

    return lax.fori_loop(0, sz.planes // 2, planes, start, unroll=2)


def pairs_kernel(
    sz, lists, counts, own, resident, early, wz, wy, wx, wyi, result, inner,
    total, arrived, t, u, scales, out1, in1, out2, in2, terms,
    send_sem, recv_sem, pass_send, pass_recv, local_sem, term_send, term_recv,
):
    me = lax.axis_index("grid")
    block = lax.axis_index("band")
    blocks = lax.axis_size("band")
    parts = sz.parts
    after = lax.rem(block + 1, blocks)
    before = lax.rem(block + blocks - 1, blocks)

    barrier = pltpu.get_barrier_semaphore()
    for o in range(1, parts):
        pl.semaphore_signal(
            barrier, inc=1, device_id=(block, lax.rem(me + o, parts)), device_id_type=MESH
        )
    for other in (after, before):
        pl.semaphore_signal(barrier, inc=1, device_id=(other, me), device_id_type=MESH)
    pl.semaphore_wait(barrier, parts + 1)

    passing = pltpu.make_async_remote_copy(
        src_ref=resident, dst_ref=arrived, send_sem=pass_send, recv_sem=pass_recv,
        device_id=(after, me), device_id_type=MESH,
    )
    passing.start()

    more = [counts[0, l] > 1 for l in range(2)]
    both = more[0] & more[1]
    firsts = [lists[0, l, 0, 0] for l in range(2)]
    seconds = [lists[0, l, 0, 1] for l in range(2)]
    firsts.append(jnp.where(more[1], lists[0, 1, 1, 0], lists[0, 0, 1, 0]))
    seconds.append(jnp.where(more[1], lists[0, 1, 1, 1], lists[0, 0, 1, 1]))
    live = (True, True, more[0] | more[1])

    def partner_of(l):
        def partner(x, c):
            if l == 0:
                return resident[seconds[l], pl.ds(x, c)]
            if l == 1:
                return arrived[seconds[l], pl.ds(x, c)]
            return jnp.where(
                more[1],
                arrived[seconds[l], pl.ds(x, c)].astype(F32),
                resident[seconds[l], pl.ds(x, c)].astype(F32),
            )

        return partner

    def send(phase, src, dst, l, write):
        copies = []
        for o in range(1, parts):
            to = lax.rem(me + o, parts)
            write(to)
            c = pltpu.make_async_remote_copy(
                src_ref=src.at[l, to], dst_ref=dst.at[l, me],
                send_sem=send_sem.at[phase, l, o], recv_sem=recv_sem.at[phase, l, o],
                device_id=(block, to), device_id_type=MESH,
            )
            c.start()
            copies.append(c)
        write(me)
        c = pltpu.make_async_copy(src.at[l, me], dst.at[l, me], local_sem.at[phase, l])
        c.start()
        copies.append(c)
        return copies

    flights = {}
    for l in range(3):
        if l == 1:
            passing.wait()
        peak = forward(
            sz, lambda x, c: own[firsts[l], pl.ds(x, c)], partner_of(l), wz, wy, t
        )
        code = code_of(peak)
        flights[0, l] = send(
            0, out1, in1, l, lambda w: forward_words(sz, t, out1.at[l], w, code)
        )
    for l in range(3):
        for c in flights[0, l]:
            c.wait()
        code = code_of(middle(sz, me, in1.at[l], wx, scales, u))
        flights[1, l] = send(
            1, out2, in2, l, lambda w: middle_words(sz, u, out2.at[l], w, code)
        )
    bands = sz.bands
    for l in range(3):
        for c in flights[1, l]:
            c.wait()

        def add(x, v, carried):
            sums = []
            for band in range(bands):
                share = jnp.where((firsts[l] == band) & live[l], v, 0.0)
                if l == 0:
                    sooner = both & (lists[0, 0, 1, 0] == band)
                    total[band, pl.ds(x, 2)] = share + jnp.where(
                        sooner, early[pl.ds(x, 2)], 0.0
                    )
                elif l == 1:
                    total[band, pl.ds(x, 2)] += share
                else:
                    sums.append(total[band, pl.ds(x, 2)] + share)
                    result[band, pl.ds(x, 2)] = sums[-1].astype(BF16)
            if l < 2:
                return carried
            carried = list(carried)
            for i in range(bands):
                mine = own[i, pl.ds(x, 2)].astype(F32)
                for k in range(bands):
                    product = (mine * sums[k]).reshape(-1, 8, sz.length)
                    carried[i * bands + k] += jnp.sum(product, axis=0)
            return tuple(carried)

        start = 0
        if l == 2:
            start = (jnp.zeros((8, sz.length), F32),) * (bands * bands)
        ended = backward(
            sz, in2.at[l], wz, wyi, scales, t, partner_of(l), add, start
        )
    for i, v in enumerate(ended):
        terms[me, i] = v
    copies = []
    for o in range(1, parts):
        c = pltpu.make_async_remote_copy(
            src_ref=terms.at[me], dst_ref=terms.at[me],
            send_sem=term_send.at[o], recv_sem=term_recv.at[o],
            device_id=(block, lax.rem(me + o, parts)), device_id_type=MESH,
        )
        c.start()
        copies.append(c)
    for c in copies:
        c.wait()
    inner[...] = sum(terms[g] for g in range(parts))


def all_pairs(sz, lists, counts, own, resident, early, wz, wy, wx, wyi):
    n = sz.length
    vmem = pl.BlockSpec(memory_space=pltpu.VMEM)
    smem = pl.BlockSpec(memory_space=pltpu.SMEM)
    coded = pltpu.VMEM((3,) + sz.coded(), I16)
    squared = sz.bands * sz.bands
    return pl.pallas_call(
        functools.partial(pairs_kernel, sz),
        out_shape=(
            jax.ShapeDtypeStruct(own.shape, BF16),
            jax.ShapeDtypeStruct((squared, 8, n), F32),
        ),
        in_specs=[smem] * 2 + [vmem] * 7,
        out_specs=(vmem, vmem),
        scratch_shapes=[
            pltpu.VMEM(own.shape, F32),
            pltpu.VMEM(own.shape, BF16),
            pltpu.VMEM((n * sz.planes, n), F32),
            pltpu.VMEM((sz.rows, n, n), F32),
            pltpu.VMEM((n, n), F32),
            coded, coded, coded, coded,
            pltpu.VMEM((sz.parts, squared, 8, n), F32),
            pltpu.SemaphoreType.DMA((2, 3, sz.parts)),
            pltpu.SemaphoreType.DMA((2, 3, sz.parts)),
            pltpu.SemaphoreType.DMA,
            pltpu.SemaphoreType.DMA,
            pltpu.SemaphoreType.DMA((2, 3)),
            pltpu.SemaphoreType.DMA((sz.parts,)),
            pltpu.SemaphoreType.DMA((sz.parts,)),
        ],
        compiler_params=pltpu.CompilerParams(
            collective_id=0, has_side_effects=True, vmem_limit_bytes=LIMIT
        ),
        name="all_pairs",
    )(lists, counts, own, resident, early, wz, wy, wx, wyi)


def extra_forward(sz, own, partner, wz, wy):
    def kernel(own_ref, partner_ref, wz_ref, wy_ref, out, t):
        peak = forward(
            sz, lambda x, c: own_ref[pl.ds(x, c)], lambda x, c: partner_ref[pl.ds(x, c)],
            wz_ref, wy_ref, t,
        )
        code = code_of(peak)
        for g in range(sz.parts):
            forward_words(sz, t, out, g, code)

    return pl.pallas_call(
        kernel,
        out_shape=jax.ShapeDtypeStruct(sz.coded(), I16),
        scratch_shapes=[pltpu.VMEM((sz.length * sz.planes, sz.length), F32)],
        compiler_params=pltpu.CompilerParams(vmem_limit_bytes=LIMIT),
        name="extra_forward",
    )(own, partner, wz, wy)


def extra_middle(sz, coded, wx):
    n = sz.length

    def kernel(coded_ref, wx_ref, out, scales, u):
        me = lax.axis_index("grid")
        code = code_of(middle(sz, me, coded_ref, wx_ref, scales, u))
        for g in range(sz.parts):
            middle_words(sz, u, out, g, code)

    return pl.pallas_call(
        kernel,
        out_shape=jax.ShapeDtypeStruct(sz.coded(), I16),
        scratch_shapes=[pltpu.VMEM((n, n), F32), pltpu.VMEM((sz.rows, n, n), F32)],
        compiler_params=pltpu.CompilerParams(vmem_limit_bytes=LIMIT),
        name="extra_middle",
    )(coded, wx)


def extra_backward(sz, coded, partner, wz, wyi):
    n = sz.length

    def kernel(coded_ref, partner_ref, wz_ref, wyi_ref, out, scales, t):
        def add(x, v, carried):
            out[pl.ds(x, 2)] = v
            return carried

        backward(
            sz, coded_ref, wz_ref, wyi_ref, scales, t,
            lambda x, c: partner_ref[pl.ds(x, c)], add,
        )

    return pl.pallas_call(
        kernel,
        out_shape=jax.ShapeDtypeStruct((sz.planes, n, n), F32),
        scratch_shapes=[pltpu.VMEM((n, n), F32), pltpu.VMEM((n * sz.planes, n), F32)],
        compiler_params=pltpu.CompilerParams(vmem_limit_bytes=LIMIT),
        name="extra_backward",
    )(coded, partner, wz, wyi)


def on_device(own, resident, pair_lists, pair_counts):
    bands, planes, length, _ = own.shape
    sz = Sizes(bands, planes, length)
    wz, wy, wx, wyi = tables(length, sz.parts)

    def one_pair(_, term):
        row = pair_lists[0, 0, 1]
        own_band = lax.dynamic_index_in_dim(own, row[0], 0, keepdims=False)
        partner = lax.dynamic_index_in_dim(resident, row[1], 0, keepdims=False)
        coded = extra_forward(sz, own_band, partner, wz, wy)
        coded = lax.all_to_all(coded, "grid", split_axis=0, concat_axis=0, tiled=True)
        coded = extra_middle(sz, coded, wx)
        coded = lax.all_to_all(coded, "grid", split_axis=0, concat_axis=0, tiled=True)
        return term + extra_backward(sz, coded, partner, wz, wyi)

    ahead = (pair_counts[0, 0] - 1) * (pair_counts[0, 1] - 1)
    early = jnp.zeros(own.shape[1:], F32)
    early = lax.fori_loop(0, ahead, one_pair, early)
    rounded, products = all_pairs(
        sz, pair_lists, pair_counts, own, resident, early, wz, wy, wx, wyi
    )
    return rounded, jnp.sum(products, axis=(1, 2)).reshape(bands, bands)


def solution(mesh):
    in_specs = (
        P("band", "grid", None, None),
        P("band", "grid", None, None),
        P("band", None, None, None),
        P("band", None),
    )
    out_specs = (P("band", "grid", None, None), P("band", None))
    return jax.shard_map(
        on_device, mesh=mesh, in_specs=in_specs, out_specs=out_specs, check_vma=False
    )
```

```python
import functools
import math

import jax
import jax.numpy as jnp
import numpy as np
import ml_dtypes
from jax import lax
from jax.experimental import pallas as pl
from jax.experimental.pallas import tpu as pltpu
from jax.sharding import PartitionSpec as P

F32 = jnp.float32
BF16 = jnp.bfloat16
I16 = jnp.int16
MESH = pl.DeviceIdType.MESH
FINE_ROWS = 4
FINE = 65000.0
TOP = 32700.0
LIMIT = 56 * 2**20


def tables(length, parts):
    k = np.arange(length)
    angles = (np.outer(k, k) % length) * (2.0 * math.pi / length)
    cas = (np.cos(angles) + np.sin(angles)) / math.sqrt(length)
    order = sorted(range(length), key=lambda i: (min(i, length - i), i))
    rows = length // parts
    perm = np.array([order[r * parts + g] for g in range(parts) for r in range(rows)])

    def split(m):
        high = m.astype(np.float32).astype(ml_dtypes.bfloat16)
        low = (m - high.astype(np.float64)).astype(np.float32).astype(ml_dtypes.bfloat16)
        return high, low

    def left(m):
        high, low = split(m)
        return np.block([[high, high], [low, np.zeros_like(low)]])

    def right(m):
        high, low = split(m)
        return np.block([[high, low], [high, np.zeros_like(low)]])

    return [
        jnp.asarray(t.astype(ml_dtypes.bfloat16))
        for t in (right(cas), left(cas[perm, :]), left(cas), left(cas[:, perm]))
    ]


def halves(v):
    high = v.astype(BF16)
    return high, (v - high.astype(F32)).astype(BF16)


def times_right(v, table):
    high, low = halves(v)
    n = v.shape[1]
    out = jnp.dot(jnp.concatenate([high, low], 1), table, preferred_element_type=F32)
    return out[:, :n] + out[:, n:]


def times_left(table, a, b):
    ah, al = halves(a)
    bh, bl = halves(b)
    rhs = jnp.concatenate(
        [jnp.concatenate([ah, bh], 1), jnp.concatenate([al, bl], 1)], 0
    )
    out = jnp.dot(table, rhs, preferred_element_type=F32)
    n = a.shape[0]
    return out[:n] + out[n:]


def tile_max(running, v):
    return jnp.maximum(running, jnp.max(jnp.abs(v).reshape(-1, 8, v.shape[-1]), axis=0))


def folded(index, length):
    return jnp.minimum(index, length - index)


def code_of(peak):
    peak = jnp.maximum(jnp.max(peak, keepdims=True), 1e-30)
    return jnp.ceil(jnp.log2(peak) * 256.0)


def size_of(code):
    return jnp.exp2(code * (1.0 / 256.0))


class Sizes:
    def __init__(self, bands, planes, length):
        self.bands = bands
        self.planes = planes
        self.length = length
        self.parts = length // planes
        self.rows = planes
        self.fine = max(1, FINE_ROWS // self.parts)
        self.all_rows = self.rows + self.fine + 1
        half = planes // 2
        self.whole = ((0, planes),)
        self.cut = ((0, half), (half, half)) if half % 16 == 0 else self.whole

    def coded(self):
        return (self.parts, self.all_rows, self.planes, self.length)


def write_words(sz, out, where, load, inverse, code, span):
    low, count = span
    some = slice(low, low + count)

    def words(v):
        return v.astype(jnp.int32).astype(I16)

    def body(r, _):
        out[where, r, some] = words(jnp.round(load(r) * inverse))
        return 0

    for r in range(sz.fine):
        scaled = load(r) * inverse
        whole = jnp.round(scaled)
        out[where, r, some] = words(whole)
        out[where, sz.rows + r, some] = words(jnp.round((scaled - whole) * FINE))
    for r in range(sz.fine, sz.fine + sz.fine % 2):
        body(r, 0)
    lax.fori_loop(sz.fine + sz.fine % 2, sz.rows, body, 0, unroll=2)
    out[where, sz.rows + sz.fine, some] = words(
        jnp.broadcast_to(code, (count, sz.length))
    )


def forward(sz, own, partner, wz, wy, t, span):
    n = sz.length

    def body(step, peak):
        x = span[0] + step * 4
        d = own(x, 4).astype(F32) * partner(x, 4).astype(F32)
        e = times_right(d.reshape(4 * n, n), wz[...])
        for h in range(2):
            a, b = 2 * h, 2 * h + 1
            f = times_left(wy[...], e[a * n : (a + 1) * n], e[b * n : (b + 1) * n])
            t[pl.ds(x + a, n, stride=sz.planes), :] = f[:, :n]
            t[pl.ds(x + b, n, stride=sz.planes), :] = f[:, n:]
            peak = tile_max(peak, f)
        return peak

    return lax.fori_loop(0, span[1] // 4, body, jnp.zeros((8, 2 * n), F32))


def forward_words(sz, t, out, where, code, span):
    inverse = TOP / size_of(code)
    base = where * (sz.rows * sz.planes)

    def load(r):
        start = pl.multiple_of(base + r * sz.planes + span[0], 8)
        return t[pl.ds(start, span[1]), :]

    write_words(sz, out, where, load, inverse, code, span)


def set_scales(sz, coded, scales, span):
    low, count = span
    for src in range(sz.parts):
        row = coded[src, sz.rows + sz.fine, low : low + count]
        first = src * sz.planes + low
        scales[first : first + count, :] = size_of(
            row.astype(jnp.int32).astype(F32)
        ) * (1.0 / TOP)


def numbers(sz, coded, src, r, is_fine, span):
    some = slice(span[0], span[0] + span[1])
    v = coded[src, r, some].astype(jnp.int32).astype(F32)
    if is_fine:
        rest = coded[src, sz.rows + r, some].astype(jnp.int32).astype(F32)
        v = v + rest * (1.0 / FINE)
    return v


def row_frequency(sz, part, r):
    return ((r * sz.parts + part + 1) // 2).astype(F32)


def column_power(sz, my, power):
    kz = folded(lax.broadcasted_iota(jnp.int32, (8, sz.length), 1), sz.length).astype(F32)
    squared = jnp.maximum(kz * kz + my * my, 1.0)
    root = jnp.sqrt(squared)
    w = root * jnp.sqrt(root)
    return (w if power > 0 else 1.0 / w)[0:1]


def middle(sz, me, coded, wx, scales, u):
    n = sz.length
    set_scales(sz, coded, scales, sz.whole[0])
    factor = 0.25 * n**1.5

    def squares():
        kx = folded(lax.broadcasted_iota(jnp.int32, (n, n), 0), n)
        kz = folded(lax.broadcasted_iota(jnp.int32, (n, n), 1), n)
        return (kx * kx + kz * kz).astype(F32)

    def pair(r, is_fine, peak):
        g = [
            jnp.concatenate(
                [
                    numbers(
                        sz, coded, src, r + h, is_fine and r + h < sz.fine, sz.whole[0]
                    )
                    for src in range(sz.parts)
                ],
                0,
            )
            * scales[...]
            for h in range(2)
        ]
        s = times_left(wx[...], g[0], g[1])
        base = squares()
        filtered = []
        my = [row_frequency(sz, me, jnp.int32(r) + h) for h in range(2)]
        for h in range(2):
            k = base + my[h] * my[h]
            k = jnp.where(k > 0.5, factor / jnp.maximum(k, 1.0), 0.0)
            filtered.append(s[:, h * n : (h + 1) * n] * k)
        back = times_left(wx[...], filtered[0], filtered[1])
        for h in range(2):
            v = back[:, h * n : (h + 1) * n] * column_power(sz, my[h], 1)
            u[r + h] = v
            peak = tile_max(peak, v)
        return peak

    peak = jnp.zeros((8, n), F32)
    for r in range(0, sz.fine, 2):
        peak = pair(r, True, peak)
    return lax.fori_loop(
        (sz.fine + 1) // 2, sz.rows // 2, lambda s, p: pair(s * 2, False, p), peak
    )


def middle_words(sz, u, out, where, code, span):
    inverse = TOP / size_of(code)

    def load(r):
        start = pl.multiple_of(where * sz.planes + span[0], 8)
        return u[r, pl.ds(start, span[1]), :]

    write_words(sz, out, where, load, inverse, code, span)


def backward(sz, coded, wz, wyi, scales, t, partner, add, span, start=0):
    n = sz.length
    low, count = span
    set_scales(sz, coded, scales, span)
    for src in range(sz.parts):

        def put(r, is_fine):
            my = row_frequency(sz, src, jnp.int32(r))
            scale = scales[src * sz.planes + low : src * sz.planes + low + 8, :][0:1]
            v = numbers(sz, coded, src, r, is_fine, span)
            first = pl.multiple_of((src * sz.rows + r) * sz.planes + low, 8)
            t[pl.ds(first, count), :] = v * (scale * column_power(sz, my, -1))

        for r in range(sz.fine):
            put(r, True)

        def body(r, _):
            put(r, False)
            return 0

        for r in range(sz.fine, sz.fine + sz.fine % 2):
            put(r, False)
        lax.fori_loop(sz.fine + sz.fine % 2, sz.rows, body, 0, unroll=2)

    def planes(step, carried):
        x = low + step * 2
        a = t[pl.ds(x, n, stride=sz.planes), :]
        b = t[pl.ds(x + 1, n, stride=sz.planes), :]
        f = times_left(wyi[...], a, b)
        v = times_right(jnp.concatenate([f[:, :n], f[:, n:]], 0), wz[...])
        return add(x, v.reshape(2, n, n) * partner(x, 2).astype(F32), carried)

    return lax.fori_loop(0, count // 2, planes, start, unroll=2)


def pairs_kernel(
    sz, lists, counts, own, resident, early, wz, wy, wx, wyi, result, inner,
    total, arrived, t, u, scales, out1, in1, out2, in2, terms,
    send_sem, recv_sem, pass_send, pass_recv, local_sem, term_send, term_recv,
):
    me = lax.axis_index("grid")
    block = lax.axis_index("band")
    blocks = lax.axis_size("band")
    parts = sz.parts
    after = lax.rem(block + 1, blocks)
    before = lax.rem(block + blocks - 1, blocks)

    barrier = pltpu.get_barrier_semaphore()
    for o in range(1, parts):
        pl.semaphore_signal(
            barrier, inc=1, device_id=(block, lax.rem(me + o, parts)), device_id_type=MESH
        )
    for other in (after, before):
        pl.semaphore_signal(barrier, inc=1, device_id=(other, me), device_id_type=MESH)
    pl.semaphore_wait(barrier, parts + 1)

    passing = pltpu.make_async_remote_copy(
        src_ref=resident, dst_ref=arrived, send_sem=pass_send, recv_sem=pass_recv,
        device_id=(after, me), device_id_type=MESH,
    )
    passing.start()

    more = [counts[0, l] > 1 for l in range(2)]
    both = more[0] & more[1]
    firsts = [lists[0, l, 0, 0] for l in range(2)]
    seconds = [lists[0, l, 0, 1] for l in range(2)]
    firsts.append(jnp.where(more[1], lists[0, 1, 1, 0], lists[0, 0, 1, 0]))
    seconds.append(jnp.where(more[1], lists[0, 1, 1, 1], lists[0, 0, 1, 1]))
    live = (True, True, more[0] | more[1])

    def partner_of(l):
        def partner(x, c):
            if l == 0:
                return resident[seconds[l], pl.ds(x, c)]
            if l == 1:
                return arrived[seconds[l], pl.ds(x, c)]
            return jnp.where(
                more[1],
                arrived[seconds[l], pl.ds(x, c)].astype(F32),
                resident[seconds[l], pl.ds(x, c)].astype(F32),
            )

        return partner

    def send(phase, src, dst, l, cut, span, write):
        copies = []
        rows = pl.ds(span[0], span[1])
        for o in range(1, parts):
            to = lax.rem(me + o, parts)
            write(to)
            c = pltpu.make_async_remote_copy(
                src_ref=src.at[l, to, :, rows], dst_ref=dst.at[l, me, :, rows],
                send_sem=send_sem.at[phase, l, cut, o],
                recv_sem=recv_sem.at[phase, l, cut, o],
                device_id=(block, to), device_id_type=MESH,
            )
            c.start()
            copies.append(c)
        write(me)
        c = pltpu.make_async_copy(
            src.at[l, me, :, rows], dst.at[l, me, :, rows], local_sem.at[phase, l, cut]
        )
        c.start()
        copies.append(c)
        return copies

    cuts = {(p, l): sz.whole for p in range(2) for l in range(3)}
    cuts[0, 0] = cuts[1, 2] = sz.cut

    flights = {}
    for l in range(3):
        if l == 1:
            passing.wait()
        for cut, span in enumerate(cuts[0, l]):
            peak = forward(
                sz, lambda x, c: own[firsts[l], pl.ds(x, c)], partner_of(l), wz, wy, t,
                span,
            )
            code = code_of(peak)
            flights[0, l, cut] = send(
                0, out1, in1, l, cut, span,
                lambda w: forward_words(sz, t, out1.at[l], w, code, span),
            )
    for l in range(3):
        for cut in range(len(cuts[0, l])):
            for c in flights[0, l, cut]:
                c.wait()
        code = code_of(middle(sz, me, in1.at[l], wx, scales, u))
        for cut, span in enumerate(cuts[1, l]):
            flights[1, l, cut] = send(
                1, out2, in2, l, cut, span,
                lambda w: middle_words(sz, u, out2.at[l], w, code, span),
            )
    bands = sz.bands
    for l in range(3):

        def add(x, v, carried):
            sums = []
            for band in range(bands):
                share = jnp.where((firsts[l] == band) & live[l], v, 0.0)
                if l == 0:
                    sooner = both & (lists[0, 0, 1, 0] == band)
                    total[band, pl.ds(x, 2)] = share + jnp.where(
                        sooner, early[pl.ds(x, 2)], 0.0
                    )
                elif l == 1:
                    total[band, pl.ds(x, 2)] += share
                else:
                    sums.append(total[band, pl.ds(x, 2)] + share)
                    result[band, pl.ds(x, 2)] = sums[-1].astype(BF16)
            if l < 2:
                return carried
            carried = list(carried)
            for i in range(bands):
                mine = own[i, pl.ds(x, 2)].astype(F32)
                for k in range(bands):
                    product = (mine * sums[k]).reshape(-1, 8, sz.length)
                    carried[i * bands + k] += jnp.sum(product, axis=0)
            return tuple(carried)

        ended = 0
        if l == 2:
            ended = (jnp.zeros((8, sz.length), F32),) * (bands * bands)
        for cut, span in enumerate(cuts[1, l]):
            for c in flights[1, l, cut]:
                c.wait()
            ended = backward(
                sz, in2.at[l], wz, wyi, scales, t, partner_of(l), add, span, ended
            )
    for i, v in enumerate(ended):
        terms[me, i] = v
    copies = []
    for o in range(1, parts):
        c = pltpu.make_async_remote_copy(
            src_ref=terms.at[me], dst_ref=terms.at[me],
            send_sem=term_send.at[o], recv_sem=term_recv.at[o],
            device_id=(block, lax.rem(me + o, parts)), device_id_type=MESH,
        )
        c.start()
        copies.append(c)
    for c in copies:
        c.wait()
    inner[...] = sum(terms[g] for g in range(parts))


def all_pairs(sz, lists, counts, own, resident, early, wz, wy, wx, wyi):
    n = sz.length
    vmem = pl.BlockSpec(memory_space=pltpu.VMEM)
    smem = pl.BlockSpec(memory_space=pltpu.SMEM)
    coded = pltpu.VMEM((3,) + sz.coded(), I16)
    squared = sz.bands * sz.bands
    return pl.pallas_call(
        functools.partial(pairs_kernel, sz),
        out_shape=(
            jax.ShapeDtypeStruct(own.shape, BF16),
            jax.ShapeDtypeStruct((squared, 8, n), F32),
        ),
        in_specs=[smem] * 2 + [vmem] * 7,
        out_specs=(vmem, vmem),
        scratch_shapes=[
            pltpu.VMEM(own.shape, F32),
            pltpu.VMEM(own.shape, BF16),
            pltpu.VMEM((n * sz.planes, n), F32),
            pltpu.VMEM((sz.rows, n, n), F32),
            pltpu.VMEM((n, n), F32),
            coded, coded, coded, coded,
            pltpu.VMEM((sz.parts, squared, 8, n), F32),
            pltpu.SemaphoreType.DMA((2, 3, 2, sz.parts)),
            pltpu.SemaphoreType.DMA((2, 3, 2, sz.parts)),
            pltpu.SemaphoreType.DMA,
            pltpu.SemaphoreType.DMA,
            pltpu.SemaphoreType.DMA((2, 3, 2)),
            pltpu.SemaphoreType.DMA((sz.parts,)),
            pltpu.SemaphoreType.DMA((sz.parts,)),
        ],
        compiler_params=pltpu.CompilerParams(
            collective_id=0, has_side_effects=True, vmem_limit_bytes=LIMIT
        ),
        name="all_pairs",
    )(lists, counts, own, resident, early, wz, wy, wx, wyi)


def extra_forward(sz, own, partner, wz, wy):
    def kernel(own_ref, partner_ref, wz_ref, wy_ref, out, t):
        peak = forward(
            sz, lambda x, c: own_ref[pl.ds(x, c)], lambda x, c: partner_ref[pl.ds(x, c)],
            wz_ref, wy_ref, t, sz.whole[0],
        )
        code = code_of(peak)
        for g in range(sz.parts):
            forward_words(sz, t, out, g, code, sz.whole[0])

    return pl.pallas_call(
        kernel,
        out_shape=jax.ShapeDtypeStruct(sz.coded(), I16),
        scratch_shapes=[pltpu.VMEM((sz.length * sz.planes, sz.length), F32)],
        compiler_params=pltpu.CompilerParams(vmem_limit_bytes=LIMIT),
        name="extra_forward",
    )(own, partner, wz, wy)


def extra_middle(sz, coded, wx):
    n = sz.length

    def kernel(coded_ref, wx_ref, out, scales, u):
        me = lax.axis_index("grid")
        code = code_of(middle(sz, me, coded_ref, wx_ref, scales, u))
        for g in range(sz.parts):
            middle_words(sz, u, out, g, code, sz.whole[0])

    return pl.pallas_call(
        kernel,
        out_shape=jax.ShapeDtypeStruct(sz.coded(), I16),
        scratch_shapes=[pltpu.VMEM((n, n), F32), pltpu.VMEM((sz.rows, n, n), F32)],
        compiler_params=pltpu.CompilerParams(vmem_limit_bytes=LIMIT),
        name="extra_middle",
    )(coded, wx)


def extra_backward(sz, coded, partner, wz, wyi):
    n = sz.length

    def kernel(coded_ref, partner_ref, wz_ref, wyi_ref, out, scales, t):
        def add(x, v, carried):
            out[pl.ds(x, 2)] = v
            return carried

        backward(
            sz, coded_ref, wz_ref, wyi_ref, scales, t,
            lambda x, c: partner_ref[pl.ds(x, c)], add, sz.whole[0],
        )

    return pl.pallas_call(
        kernel,
        out_shape=jax.ShapeDtypeStruct((sz.planes, n, n), F32),
        scratch_shapes=[pltpu.VMEM((n, n), F32), pltpu.VMEM((n * sz.planes, n), F32)],
        compiler_params=pltpu.CompilerParams(vmem_limit_bytes=LIMIT),
        name="extra_backward",
    )(coded, partner, wz, wyi)


def on_device(own, resident, pair_lists, pair_counts):
    bands, planes, length, _ = own.shape
    sz = Sizes(bands, planes, length)
    wz, wy, wx, wyi = tables(length, sz.parts)

    def one_pair(step, term):
        row = pair_lists[0, 0, 1 + step]
        own_band = lax.dynamic_index_in_dim(own, row[0], 0, keepdims=False)
        partner = lax.dynamic_index_in_dim(resident, row[1], 0, keepdims=False)
        coded = extra_forward(sz, own_band, partner, wz, wy)
        coded = lax.all_to_all(coded, "grid", split_axis=0, concat_axis=0, tiled=True)
        coded = extra_middle(sz, coded, wx)
        coded = lax.all_to_all(coded, "grid", split_axis=0, concat_axis=0, tiled=True)
        return term + extra_backward(sz, coded, partner, wz, wyi)

    ahead = (pair_counts[0, 0] - 1) * (pair_counts[0, 1] - 1)
    early = jnp.zeros(own.shape[1:], F32)
    early = lax.fori_loop(0, ahead, one_pair, early)
    rounded, products = all_pairs(
        sz, pair_lists, pair_counts, own, resident, early, wz, wy, wx, wyi
    )
    return rounded, jnp.sum(products, axis=(1, 2)).reshape(bands, bands)


def solution(mesh):
    in_specs = (
        P("band", "grid", None, None),
        P("band", "grid", None, None),
        P("band", None, None, None),
        P("band", None),
    )
    out_specs = (P("band", "grid", None, None), P("band", None))
    return jax.shard_map(
        on_device, mesh=mesh, in_specs=in_specs, out_specs=out_specs, check_vma=False
    )
```
